32 devices in a mesh: group: 2 (over x), tm: 2 (over core), space: 8 (over z, y).
Axes of the slice: x: 2, y: 2, z: 4, core: 2. Of those that a mesh axis runs over, the one named last changes fastest.
Arguments:
- start_old: float32 [4, 3, 1024, 1024], P(('group', 'tm'), None, 'space'), parts along dimension 0, may hold values from -3 to 3
- incoming: float32 [6, 512, 512], P('group', 'space'), parts along dimension 0, may hold values from -3 to 3
Outputs:
- new_states: float32 [4, 3, 1024, 1024], P(('group', 'tm'), None, 'space'), parts along dimension 0
The draws below stay inside these ranges and needn't reach their ends.
There are 2 independent parts, one for each index of `group`. The reference program is written for one: setup_inputs(seed, part) draws one part's arguments, and reference() takes and returns one part's arrays. A program takes and returns all parts, laid end to end along the dimension named above; each array names one. Nothing has to cross between parts.
All inputs are finite; a program needn't handle non-finite values.
Results may differ from the reference program's by a relative error of at most 0.0001.
Values sent between devices are 32-bit elements; how exact they have to be, the bound alone decides.
A program may use at most 192 MiB of HBM per device.

```python
import math
import jax
import jax.numpy as jnp
from jax import lax

NC = 512
RATIO = 2
STEPS = 2
SLICES = 2
NF = 1024


def steps_of(stream_key, shape, pieces, low, high):
    gain = 1.0
    for dim, shards_of in pieces:
        steps = jax.random.uniform(jax.random.fold_in(jax.random.fold_in(stream_key, 6), dim), (shards_of,), jnp.float32, low / len(pieces), high / len(pieces))
        gain = gain * jnp.repeat(jnp.exp(steps), shape[dim] // shards_of).reshape((-1,) + (1,) * (len(shape) - 1 - dim))
    return gain


def centred(own_key, shape, scale, most, split=(), kind=jnp.bfloat16):
    result = jax.random.normal(own_key, shape, jnp.float32) * scale
    if len(split) > 0:
        result = steps_of(own_key, shape, split, -0.22, 0.18) * result
    return jnp.clip(result, min=-most, max=most).astype(kind)


def setup_inputs(seed: int = 0, part: int = 0) -> dict:
    streams_of = jax.random.split(jax.random.key(seed), 3)
    part_splits = jax.random.split(jax.random.fold_in(streams_of[2], part), 3)
    return {
        "start_old": centred(part_splits[0], (SLICES, 3, NF, NF), 0.5, 3.0, ((0, 2), (2, 8)), jnp.float32),
        "incoming": centred(part_splits[1], (3, NC, NC), 0.5, 3.0, ((1, 8),), jnp.float32),
    }


TIME_STEP = 0.25
CORIOLIS = 0.5
GRAVITY = 1.0
MEAN_DEPTH = 1.0

def slope_east(field):
    return 0.5 * (jnp.roll(field, -1, -1) - jnp.roll(field, 1, -1))

def slope_north(field):
    return 0.5 * (jnp.roll(field, -1, -2) - jnp.roll(field, 1, -2))

def tendency(state):
    column_depth = MEAN_DEPTH + state[0]
    flux_east = column_depth * state[1]
    flux_north = column_depth * state[2]
    height, wind_east, wind_north = (state[0], state[1], state[2])
    rate_height = -(slope_east(flux_east) + slope_north(flux_north))
    rate_east = -(wind_east * slope_east(wind_east) + wind_north * slope_north(wind_east)) + CORIOLIS * wind_north - GRAVITY * slope_east(height)
    rate_north = -(wind_east * slope_east(wind_north) + wind_north * slope_north(wind_north)) - CORIOLIS * wind_east - GRAVITY * slope_north(height)
    return jnp.stack([rate_height, rate_east, rate_north])

def heun(state):
    first = state + TIME_STEP * tendency(state)
    return 0.5 * (state + first + TIME_STEP * tendency(first))

def restrict(field):
    fields, rows, cols = field.shape
    return field.reshape(fields, rows // RATIO, RATIO, cols // RATIO, RATIO).mean(axis=(2, 4))

def prolong(field):
    return jnp.repeat(jnp.repeat(field, RATIO, axis=-2), RATIO, axis=-1)

def wavenumbers(count, offset):
    index = offset + jnp.arange(count, dtype=jnp.int32)
    half = NC // 2
    shifted = jnp.where(index < half, index, index - NC)
    shifted = jnp.where(index == half, 0, shifted)
    return shifted.astype(jnp.float32) * (2.0 * math.pi / (NC * RATIO))

def apply_operator(real_part, imag_part, wave_east, wave_north):
    mixed_real = wave_east * real_part[1] + wave_north * real_part[2]
    mixed_imag = wave_east * imag_part[1] + wave_north * imag_part[2]
    height_real = MEAN_DEPTH * mixed_imag
    height_imag = -MEAN_DEPTH * mixed_real
    east_real = GRAVITY * wave_east * imag_part[0] + CORIOLIS * real_part[2]
    east_imag = -GRAVITY * wave_east * real_part[0] + CORIOLIS * imag_part[2]
    north_real = GRAVITY * wave_north * imag_part[0] - CORIOLIS * real_part[1]
    north_imag = -GRAVITY * wave_north * real_part[0] - CORIOLIS * imag_part[1]
    return (jnp.stack([height_real, east_real, north_real]), jnp.stack([height_imag, east_imag, north_imag]))

def propagate(spectra, wave_east, wave_north, slices):
    duration = slices * (STEPS * TIME_STEP)
    omega = jnp.sqrt(CORIOLIS * CORIOLIS + GRAVITY * MEAN_DEPTH * (wave_east * wave_east + wave_north * wave_north))
    sine_term = jnp.sin(omega * duration) / omega
    versine_term = (1.0 - jnp.cos(omega * duration)) / (omega * omega)
    once_real, once_imag = apply_operator(spectra[0], spectra[1], wave_east, wave_north)
    twice_real, twice_imag = apply_operator(once_real, once_imag, wave_east, wave_north)
    return jnp.stack([spectra[0] + sine_term * once_real + versine_term * twice_real, spectra[1] + sine_term * once_imag + versine_term * twice_imag])

def spectrum(field):
    transformed = jnp.fft.fft2(field)
    return jnp.stack([jnp.real(transformed), jnp.imag(transformed)])

def reference(start_old, incoming):
    wave_east = wavenumbers(NC, 0)[None, :]
    wave_north = wavenumbers(NC, 0)[:, None]
    carried = jnp.zeros((2, 3, NC, NC), jnp.float32)
    results = []
    for slice_index in range(SLICES):
        fine = start_old[slice_index]
        for step_index in range(STEPS):
            fine = heun(fine)
        coarse_fine = restrict(fine)
        drift = restrict(start_old[slice_index])
        if slice_index == 0:
            drift = drift - incoming
        forcing = spectrum(coarse_fine) - propagate(spectrum(drift), wave_east, wave_north, 1.0)
        carried = propagate(carried, wave_east, wave_north, 1.0) + forcing
        coarse_new = jnp.real(jnp.fft.ifft2(lax.complex(carried[0], carried[1])))
        results.append(fine + prolong(coarse_new - coarse_fine))
    return jnp.stack(results)
```

```python
import math

import jax
import jax.numpy as jnp
import numpy as np
from jax import lax
from jax.experimental import pallas as pl
from jax.experimental.pallas import tpu as pltpu
from jax.sharding import PartitionSpec as P

RATIO = 2
STEPS = 2
TIME_STEP = 0.25
CORIOLIS = 0.5
HALO = 8
HIGH = lax.Precision.HIGH


def dot(spec, a, b):
    return jnp.einsum(spec, a, b, precision=HIGH, preferred_element_type=jnp.float32)


def tables(nc, parts):
    half, rows = nc // 2, nc // parts
    x = np.arange(nc)
    angle = 2.0 * math.pi / nc * (np.outer(np.arange(half), x) % nc)
    real, imag = np.cos(angle), -np.sin(angle)
    imag[0] = (-1.0) ** x
    forward = np.stack([real, imag])
    wide = 0.5 * np.repeat(forward, RATIO, axis=2)

    angle = 2.0 * math.pi / nc * (np.outer(x, x) % nc)
    cos, sin = np.cos(angle), np.sin(angle)
    along = np.stack([np.stack([cos, -sin], 1), np.stack([sin, cos], 1)])
    back = np.stack([np.stack([cos, sin], 1), np.stack([-sin, cos], 1)])
    along = along.reshape(2, parts, rows, 2 * nc).transpose(1, 0, 2, 3).reshape(2 * nc, 2 * nc)
    back = back.reshape(2 * nc, 2, parts, rows).transpose(0, 2, 1, 3).reshape(2 * nc, 2 * nc)

    scale = np.full((1, half, 1), 2.0 / (nc * nc))
    scale[:, 0] = 1.0 / (nc * nc)
    inverse = np.repeat(forward * scale, RATIO, axis=2)

    index = np.where(x < half, x, x - nc)
    index = np.where(x == half, 0, index)
    wave = index * (2.0 * math.pi / (nc * RATIO))
    omega = np.sqrt(CORIOLIS**2 + wave[:half, None] ** 2 + wave[None, :] ** 2)
    duration = STEPS * TIME_STEP
    sine = np.sin(omega * duration) / omega
    versine = (1.0 - np.cos(omega * duration)) / omega**2
    single = lambda a: np.asarray(a, np.float32)
    return [single(a) for a in (forward, wide, along, back, inverse, wave, sine, versine)]


def tendency(window):
    width = window[0].shape[-1]
    mid = [a[8:16] for a in window]
    south = [a[7:15] for a in window]
    north = [a[9:17] for a in window]
    west = [pltpu.roll(a, 1, 1) for a in mid]
    east = [pltpu.roll(a, width - 1, 1) for a in mid]
    _, u, v = mid
    flux = (1.0 + east[0]) * east[1] - (1.0 + west[0]) * west[1]
    flux = flux + ((1.0 + north[0]) * north[2] - (1.0 + south[0]) * south[2])
    half_u, half_v = 0.5 * u, 0.5 * v
    rate_u = CORIOLIS * v - (
        half_u * (east[1] - west[1]) + half_v * (north[1] - south[1]) + 0.5 * (east[0] - west[0])
    )
    rate_v = -(CORIOLIS * u) - (
        half_u * (east[2] - west[2]) + half_v * (north[2] - south[2]) + 0.5 * (north[0] - south[0])
    )
    return mid, (-0.5 * flux, rate_u, rate_v)


def heun_kernel(before, state, after, fine, now, first):
    rows = state.shape[1]
    blocks = (rows + 2 * HALO) // 8
    for f in range(3):
        now[f, 8:16] = before[f]
        now[f, 16 : 16 + rows] = state[f]
        now[f, 16 + rows : 24 + rows] = after[f]

    def window(ref, block):
        at = pl.multiple_of(block * 8, 8)
        return [ref[f, pl.ds(at, 24)] for f in range(3)]

    def predict(block, _):
        mid, rate = tendency(window(now, block))
        at = pl.multiple_of(block * 8 + 8, 8)
        for f in range(3):
            first[f, pl.ds(at, 8)] = mid[f] + TIME_STEP * rate[f]
        return 0

    def correct(out, shift):
        def body(block, _):
            mid, rate = tendency(window(first, block))
            at = pl.multiple_of(block * 8 + 8, 8)
            to = pl.multiple_of(block * 8 + 8 - shift, 8)
            for f in range(3):
                out[f, pl.ds(to, 8)] = 0.5 * (now[f, pl.ds(at, 8)] + mid[f] + TIME_STEP * rate[f])
            return 0

        return body

    for step in range(STEPS):
        lax.fori_loop(0, blocks, predict, 0)
        if step < STEPS - 1:
            lax.fori_loop(0, blocks, correct(now, 0), 0)
        else:
            lax.fori_loop(1, blocks - 1, correct(fine, 16), 0)


def heun(before, state, after):
    fields, rows, width = state.shape
    vmem = pl.BlockSpec(memory_space=pltpu.VMEM)
    padded = pltpu.VMEM((fields, rows + 4 * HALO, width), jnp.float32)
    return pl.pallas_call(
        heun_kernel,
        out_shape=jax.ShapeDtypeStruct(state.shape, jnp.float32),
        in_specs=[vmem] * 3,
        out_specs=vmem,
        scratch_shapes=[padded, padded],
        compiler_params=pltpu.CompilerParams(vmem_limit_bytes=24 << 20),
        cost_estimate=pl.CostEstimate(
            flops=200 * rows * width, bytes_accessed=24 * rows * width, transcendentals=0
        ),
    )(before, state, after)


def apply_operator(s, wave_east, wave_north):
    turn = lambda a: jnp.stack([a[:, 1], -a[:, 0]], 1)
    h, u, v = s
    return (
        turn(wave_east * u + wave_north * v),
        wave_east * turn(h) + CORIOLIS * v,
        wave_north * turn(h) - CORIOLIS * u,
    )


def propagate(s, wave_east, wave_north, sine, versine):
    once = apply_operator(s, wave_east, wave_north)
    twice = apply_operator(once, wave_east, wave_north)
    return jnp.stack([a + sine * b + versine * c for a, b, c in zip(s, once, twice)])


def shards(start_old, incoming):
    size, slices = lax.axis_size("space"), lax.axis_size("tm")
    state = start_old[0]
    _, fine_rows, width = state.shape
    rows, nc = incoming.shape[1:]
    half = nc // 2
    count = half // size
    forward, wide, along, back, inverse, wave, sine, versine = tables(nc, size)
    pairs = np.repeat(np.eye(rows, dtype=np.float32), RATIO, axis=1)

    up = [(i, (i + 1) % size) for i in range(size)]
    down = [(j, i) for i, j in up]
    before = lax.ppermute(state[:, fine_rows - HALO :], "space", up)
    after = lax.ppermute(state[:, :HALO], "space", down)

    is_first = (lax.axis_index("tm") == 0).astype(jnp.float32)
    start_rows = dot("yY,fYx->fyx", 0.5 * pairs, state)
    drift = dot("ckx,fyx->ckfy", wide, start_rows)
    drift = drift - dot("ckx,fyx->ckfy", forward, is_first * incoming)

    fine = heun(before, state, after)
    coarse_rows = dot("yY,fYx->fyx", 0.5 * pairs, fine)
    coarse = dot("ckx,fyx->ckfy", wide, coarse_rows)
    route = [(i, i + 1) for i in range(slices - 1)]
    gap = lax.ppermute(coarse, "tm", route) - drift

    gap = gap.reshape(2, size, count, 3, rows).transpose(1, 3, 2, 0, 4)
    gap = gap.reshape(size, 3 * count, 2 * rows)
    piece = lax.all_to_all(gap, "space", 0, 0)
    spectra = dot("imy,iyq->mq", piece, along.reshape(size, 2 * rows, 2 * nc))
    spectra = spectra.reshape(3, count, 2, nc)

    mine = lax.axis_index("space") * count
    cut = lambda a: lax.dynamic_slice_in_dim(jnp.asarray(a), mine, count, 0)
    wave_east = cut(wave[:half])[:, None, None]
    wave_north = wave[None, None, :]
    factors = (wave_east, wave_north, cut(sine)[:, None, :], cut(versine)[:, None, :])
    change = propagate(spectra, *factors)
    for _ in range(slices - 1):
        change = propagate(spectra + lax.ppermute(change, "tm", route), *factors)

    change = change.reshape(3 * count, 2 * nc)
    moved = dot("mq,qiy->imy", change, back.reshape(2 * nc, size, 2 * rows))
    moved = lax.all_to_all(moved, "space", 0, 0)
    moved = moved.reshape(size, 3, count, 2, rows).transpose(1, 4, 3, 0, 2)
    moved = moved.reshape(3, rows, nc)
    moved = dot("yY,fyk->fYk", pairs, moved)
    result = fine + dot("fYk,kx->fYx", moved, inverse.reshape(nc, width))
    return result[None]


def solution(mesh):
    placed = (P(("group", "tm"), None, "space", None), P("group", "space", None))
    return jax.shard_map(
        shards,
        mesh=mesh,
        in_specs=placed,
        out_specs=P(("group", "tm"), None, "space", None),
        check_vma=False,
    )
```

```python
import functools
import math

import jax
import jax.numpy as jnp
import numpy as np
from jax import lax
from jax.experimental import pallas as pl
from jax.experimental.pallas import tpu as pltpu
from jax.sharding import PartitionSpec as P

RATIO = 2
STEPS = 2
TIME_STEP = 0.25
CORIOLIS = 0.5
HALO = 8
MESH = pl.DeviceIdType.MESH
HIGH = lax.Precision.HIGH


def dot(spec, a, b):
    return jnp.einsum(spec, a, b, precision=HIGH, preferred_element_type=jnp.float32)


def halves(table):
    high = table.astype(jnp.bfloat16)
    return high, (table - high.astype(np.float32)).astype(jnp.bfloat16)


def split_dot(spec, a, table):
    high = lax.reduce_precision(a, 8, 7)
    low = (a - high).astype(jnp.bfloat16)
    high = high.astype(jnp.bfloat16)
    table_high, table_low = halves(table)
    one = lambda x, t: jnp.einsum(spec, x, t, preferred_element_type=jnp.float32)
    return one(high, table_high) + (one(low, table_high) + one(high, table_low))


def tables(nc, parts):
    half, rows = nc // 2, nc // parts
    x = np.arange(nc)
    angle = 2.0 * math.pi / nc * (np.outer(np.arange(half), x) % nc)
    real, imag = np.cos(angle), -np.sin(angle)
    imag[0] = (-1.0) ** x
    forward = np.stack([real, imag])
    wide = 0.5 * np.repeat(forward, RATIO, axis=2)

    angle = 2.0 * math.pi / nc * (np.outer(x, x) % nc)
    cos, sin = np.cos(angle), np.sin(angle)
    along = np.stack([np.stack([cos, -sin], 1), np.stack([sin, cos], 1)])
    back = np.stack([np.stack([cos, sin], 1), np.stack([-sin, cos], 1)])
    along = along.reshape(2, parts, rows, 2 * nc).transpose(1, 0, 2, 3).reshape(2 * nc, 2 * nc)
    back = back.reshape(2 * nc, 2, parts, rows).transpose(0, 2, 1, 3).reshape(2 * nc, 2 * nc)

    scale = np.full((1, half, 1), 2.0 / (nc * nc))
    scale[:, 0] = 1.0 / (nc * nc)
    inverse = np.repeat(forward * scale, RATIO, axis=2)

    index = np.where(x < half, x, x - nc)
    index = np.where(x == half, 0, index)
    wave = index * (2.0 * math.pi / (nc * RATIO))
    omega = np.sqrt(CORIOLIS**2 + wave[:half, None] ** 2 + wave[None, :] ** 2)
    duration = STEPS * TIME_STEP
    sine = np.sin(omega * duration) / omega
    versine = (1.0 - np.cos(omega * duration)) / omega**2
    single = lambda a: np.asarray(a, np.float32)
    return [single(a) for a in (forward, wide, along, back, inverse, wave, sine, versine)]


def tendency(window):
    width = window[0].shape[-1]
    mid = [a[8:16] for a in window]
    south = [a[7:15] for a in window]
    north = [a[9:17] for a in window]
    west = [pltpu.roll(a, 1, 1) for a in mid]
    east = [pltpu.roll(a, width - 1, 1) for a in mid]
    _, u, v = mid
    flux = (1.0 + east[0]) * east[1] - (1.0 + west[0]) * west[1]
    flux = flux + ((1.0 + north[0]) * north[2] - (1.0 + south[0]) * south[2])
    half_u, half_v = 0.5 * u, 0.5 * v
    rate_u = CORIOLIS * v - (
        half_u * (east[1] - west[1]) + half_v * (north[1] - south[1]) + 0.5 * (east[0] - west[0])
    )
    rate_v = -(CORIOLIS * u) - (
        half_u * (east[2] - west[2]) + half_v * (north[2] - south[2]) + 0.5 * (north[0] - south[0])
    )
    return mid, (-0.5 * flux, rate_u, rate_v)


def rows_at(row):
    return row if isinstance(row, int) else pl.multiple_of(row, 8)


def greet(peers):
    barrier = pltpu.get_barrier_semaphore()
    for peer in peers:
        pl.semaphore_signal(barrier, inc=1, device_id={"space": peer}, device_id_type=MESH)
    pl.semaphore_wait(barrier, len(peers))


def heun_kernel(size, state, fine, now, first, send, recv):
    rows = state.shape[1]
    blocks = (rows + 2 * HALO) // 8
    me = lax.axis_index("space")
    after, before = lax.rem(me + 1, size), lax.rem(me + size - 1, size)
    greet((after, before))
    copies = [
        pltpu.make_async_remote_copy(
            src_ref=state.at[:, pl.ds(source, HALO)],
            dst_ref=now.at[:, pl.ds(target, HALO)],
            send_sem=send.at[n],
            recv_sem=recv.at[n],
            device_id={"space": peer},
            device_id_type=MESH,
        )
        for n, (source, target, peer) in enumerate(
            ((rows - HALO, 8, after), (0, 16 + rows, before))
        )
    ]
    for copy in copies:
        copy.start()
    pad = jnp.zeros((HALO, state.shape[2]), jnp.float32)
    for f in range(3):
        now[f, 16 : 16 + rows] = state[f]
        for ref in (now, first):
            ref[f, 0:8] = pad
            ref[f, 24 + rows : 32 + rows] = pad

    def window(ref, block):
        at = rows_at(block * 8)
        return [ref[f, pl.ds(at, 24)] for f in range(3)]

    def predict(block, _):
        mid, rate = tendency(window(now, block))
        at = rows_at(block * 8 + 8)
        for f in range(3):
            first[f, pl.ds(at, 8)] = mid[f] + TIME_STEP * rate[f]
        return 0

    def correct(out, shift):
        def body(block, _):
            mid, rate = tendency(window(first, block))
            at = rows_at(block * 8 + 8)
            to = rows_at(block * 8 + 8 - shift)
            for f in range(3):
                out[f, pl.ds(to, 8)] = 0.5 * (now[f, pl.ds(at, 8)] + mid[f] + TIME_STEP * rate[f])
            return 0

        return body

    for step in range(STEPS):
        if step == 0:
            lax.fori_loop(2, blocks - 2, predict, 0)
            for copy in copies:
                copy.wait()
            for block in (0, 1, blocks - 2, blocks - 1):
                predict(block, 0)
        else:
            lax.fori_loop(0, blocks, predict, 0)
        if step < STEPS - 1:
            lax.fori_loop(0, blocks, correct(now, 0), 0)
        else:
            lax.fori_loop(1, blocks - 1, correct(fine, 16), 0)


def heun(state, size):
    fields, rows, width = state.shape
    vmem = pl.BlockSpec(memory_space=pltpu.VMEM)
    padded = pltpu.VMEM((fields, rows + 4 * HALO, width), jnp.float32)
    return pl.pallas_call(
        functools.partial(heun_kernel, size),
        out_shape=jax.ShapeDtypeStruct(state.shape, jnp.float32),
        in_specs=[vmem],
        out_specs=vmem,
        scratch_shapes=[padded, padded] + [pltpu.SemaphoreType.DMA((2,))] * 2,
        compiler_params=pltpu.CompilerParams(
            collective_id=0, has_side_effects=True, vmem_limit_bytes=24 << 20
        ),
        cost_estimate=pl.CostEstimate(
            flops=200 * rows * width, bytes_accessed=24 * rows * width, transcendentals=0
        ),
    )(state)


def exchange_kernel(size, blocks, out, landed, send, recv):
    me = lax.axis_index("space")
    peers = [lax.rem(me + d, size) for d in range(1, size)]
    greet(peers)
    copies = [
        pltpu.make_async_remote_copy(
            src_ref=blocks.at[peer],
            dst_ref=landed.at[me],
            send_sem=send.at[n],
            recv_sem=recv.at[n],
            device_id={"space": peer},
            device_id_type=MESH,
        )
        for n, peer in enumerate(peers)
    ]
    for copy in copies:
        copy.start()
    out[me] = blocks[me]
    for n, copy in enumerate(copies):
        copy.wait()
        origin = lax.rem(me + size - 1 - n, size)
        out[origin] = landed[origin]


def exchange(blocks, size, number):
    vmem = pl.BlockSpec(memory_space=pltpu.VMEM)
    return pl.pallas_call(
        functools.partial(exchange_kernel, size),
        out_shape=jax.ShapeDtypeStruct(blocks.shape, jnp.float32),
        in_specs=[vmem],
        out_specs=vmem,
        scratch_shapes=[pltpu.VMEM(blocks.shape, jnp.float32)]
        + [pltpu.SemaphoreType.DMA((size - 1,))] * 2,
        compiler_params=pltpu.CompilerParams(
            collective_id=number, has_side_effects=True, vmem_limit_bytes=16 << 20
        ),
        cost_estimate=pl.CostEstimate(
            flops=0, bytes_accessed=30 * blocks.size, transcendentals=0
        ),
    )(blocks)


def apply_operator(s, wave_east, wave_north):
    turn = lambda a: jnp.stack([a[:, 1], -a[:, 0]], 1)
    h, u, v = s
    return (
        turn(wave_east * u + wave_north * v),
        wave_east * turn(h) + CORIOLIS * v,
        wave_north * turn(h) - CORIOLIS * u,
    )


def propagate(s, wave_east, wave_north, sine, versine):
    once = apply_operator(s, wave_east, wave_north)
    twice = apply_operator(once, wave_east, wave_north)
    return jnp.stack([a + sine * b + versine * c for a, b, c in zip(s, once, twice)])


def shards(start_old, incoming):
    size, slices = lax.axis_size("space"), lax.axis_size("tm")
    state = start_old[0]
    width = state.shape[2]
    rows, nc = incoming.shape[1:]
    half = nc // 2
    count = half // size
    forward, wide, along, back, inverse, wave, sine, versine = tables(nc, size)
    pairs = np.repeat(np.eye(rows, dtype=np.float32), RATIO, axis=1)

    is_first = (lax.axis_index("tm") == 0).astype(jnp.float32)
    start_rows = dot("yY,fYx->fyx", 0.5 * pairs, state)
    drift = dot("ckx,fyx->ckfy", wide, start_rows)
    drift = drift - dot("ckx,fyx->ckfy", forward, is_first * incoming)

    fine = heun(state, size)
    coarse_rows = dot("yY,fYx->fyx", 0.5 * pairs, fine)
    coarse = dot("ckx,fyx->ckfy", wide, coarse_rows)
    route = [(i, i + 1) for i in range(slices - 1)]
    gap = lax.ppermute(coarse, "tm", route) - drift

    gap = gap.reshape(2, size, count, 3, rows).transpose(1, 3, 2, 0, 4)
    gap = gap.reshape(size, 3 * count, 2 * rows)
    piece = exchange(gap, size, 1)
    spectra = split_dot("imy,iyq->mq", piece, along.reshape(size, 2 * rows, 2 * nc))
    spectra = spectra.reshape(3, count, 2, nc)

    mine = lax.axis_index("space") * count
    cut = lambda a: lax.dynamic_slice_in_dim(jnp.asarray(a), mine, count, 0)
    wave_east = cut(wave[:half])[:, None, None]
    wave_north = wave[None, None, :]
    factors = (wave_east, wave_north, cut(sine)[:, None, :], cut(versine)[:, None, :])
    change = propagate(spectra, *factors)
    for _ in range(slices - 1):
        change = propagate(spectra + lax.ppermute(change, "tm", route), *factors)

    change = change.reshape(3 * count, 2 * nc)
    moved = split_dot("mq,qiy->imy", change, back.reshape(2 * nc, size, 2 * rows))
    moved = exchange(moved, size, 2)
    moved = moved.reshape(size, 3, count, 2, rows).transpose(1, 4, 3, 0, 2)
    moved = moved.reshape(3, rows, nc)
    moved = dot("yY,fyk->fYk", pairs, moved)
    result = fine + dot("fYk,kx->fYx", moved, inverse.reshape(nc, width))
    return result[None]


def solution(mesh):
    placed = (P(("group", "tm"), None, "space", None), P("group", "space", None))
    return jax.shard_map(
        shards,
        mesh=mesh,
        in_specs=placed,
        out_specs=P(("group", "tm"), None, "space", None),
        check_vma=False,
    )
```

```python
import functools
import math

import jax
import jax.numpy as jnp
import numpy as np
from jax import lax
from jax.experimental import pallas as pl
from jax.experimental.pallas import tpu as pltpu
from jax.sharding import PartitionSpec as P

RATIO = 2
STEPS = 2
TIME_STEP = 0.25
CORIOLIS = 0.5
HALO = 8
MESH = pl.DeviceIdType.MESH


def halves(table):
    high = table.astype(jnp.bfloat16)
    return high, (table - high.astype(np.float32)).astype(jnp.bfloat16)


def split(a):
    high = a.astype(jnp.bfloat16)
    return high, (a - high.astype(jnp.float32)).astype(jnp.bfloat16)


def dot(a, b, sides=(1, 0)):
    dims = (((sides[0],), (sides[1],)), ((), ()))
    return lax.dot_general(a, b, dims, preferred_element_type=jnp.float32)


def tables(nc, parts):
    half, rows = nc // 2, nc // parts
    x = np.arange(nc)
    angle = 2.0 * math.pi / nc * (np.outer(np.arange(half), x) % nc)
    real, imag = np.cos(angle), -np.sin(angle)
    imag[0] = (-1.0) ** x
    forward = np.stack([real, imag])
    wide = 0.5 * np.repeat(forward, RATIO, axis=2)

    angle = 2.0 * math.pi / nc * (np.outer(x, x) % nc)
    cos, sin = np.cos(angle), np.sin(angle)
    along = np.stack([np.stack([cos, -sin], 1), np.stack([sin, cos], 1)])
    back = np.stack([np.stack([cos, sin], 1), np.stack([-sin, cos], 1)])
    along = along.reshape(2, parts, rows, 2 * nc).transpose(1, 0, 2, 3).reshape(2 * nc, 2 * nc)
    back = back.reshape(2 * nc, 2, parts, rows).transpose(0, 2, 1, 3).reshape(2 * nc, 2 * nc)

    scale = np.full((1, half, 1), 2.0 / (nc * nc))
    scale[:, 0] = 1.0 / (nc * nc)
    inverse = np.repeat(forward * scale, RATIO, axis=2)

    index = np.where(x < half, x, x - nc)
    index = np.where(x == half, 0, index)
    wave = index * (2.0 * math.pi / (nc * RATIO))
    omega = np.sqrt(CORIOLIS**2 + wave[:half, None] ** 2 + wave[None, :] ** 2)
    duration = STEPS * TIME_STEP
    sine = np.sin(omega * duration) / omega
    versine = (1.0 - np.cos(omega * duration)) / omega**2
    single = lambda a: np.asarray(a, np.float32)
    return [single(a) for a in (forward, wide, along, back, inverse, wave, sine, versine)]


def tendency(window):
    width = window[0].shape[-1]
    mid = [a[8:16] for a in window]
    south = [a[7:15] for a in window]
    north = [a[9:17] for a in window]
    west = [pltpu.roll(a, 1, 1) for a in mid]
    east = [pltpu.roll(a, width - 1, 1) for a in mid]
    _, u, v = mid
    flux = (1.0 + east[0]) * east[1] - (1.0 + west[0]) * west[1]
    flux = flux + ((1.0 + north[0]) * north[2] - (1.0 + south[0]) * south[2])
    half_u, half_v = 0.5 * u, 0.5 * v
    rate_u = CORIOLIS * v - (
        half_u * (east[1] - west[1]) + half_v * (north[1] - south[1]) + 0.5 * (east[0] - west[0])
    )
    rate_v = -(CORIOLIS * u) - (
        half_u * (east[2] - west[2]) + half_v * (north[2] - south[2]) + 0.5 * (north[0] - south[0])
    )
    return mid, (-0.5 * flux, rate_u, rate_v)


def rows_at(row):
    return row if isinstance(row, int) else pl.multiple_of(row, 8)


def greet(peers):
    barrier = pltpu.get_barrier_semaphore()
    for peer in peers:
        pl.semaphore_signal(barrier, inc=1, device_id={"space": peer}, device_id_type=MESH)
    pl.semaphore_wait(barrier, len(peers))


def heun_kernel(size, state, fine, now, first, send, recv):
    rows = state.shape[1]
    blocks = (rows + 2 * HALO) // 8
    me = lax.axis_index("space")
    after, before = lax.rem(me + 1, size), lax.rem(me + size - 1, size)
    greet((after, before))
    copies = [
        pltpu.make_async_remote_copy(
            src_ref=state.at[:, pl.ds(source, HALO)],
            dst_ref=now.at[:, pl.ds(target, HALO)],
            send_sem=send.at[n],
            recv_sem=recv.at[n],
            device_id={"space": peer},
            device_id_type=MESH,
        )
        for n, (source, target, peer) in enumerate(
            ((rows - HALO, 8, after), (0, 16 + rows, before))
        )
    ]
    for copy in copies:
        copy.start()
    pad = jnp.zeros((HALO, state.shape[2]), jnp.float32)
    for f in range(3):
        now[f, 16 : 16 + rows] = state[f]
        for ref in (now, first):
            ref[f, 0:8] = pad
            ref[f, 24 + rows : 32 + rows] = pad

    def window(ref, block):
        at = rows_at(block * 8)
        return [ref[f, pl.ds(at, 24)] for f in range(3)]

    def predict(block, _):
        mid, rate = tendency(window(now, block))
        at = rows_at(block * 8 + 8)
        for f in range(3):
            first[f, pl.ds(at, 8)] = mid[f] + TIME_STEP * rate[f]
        return 0

    def correct(out, shift):
        def body(block, _):
            mid, rate = tendency(window(first, block))
            at = rows_at(block * 8 + 8)
            to = rows_at(block * 8 + 8 - shift)
            for f in range(3):
                out[f, pl.ds(to, 8)] = 0.5 * (now[f, pl.ds(at, 8)] + mid[f] + TIME_STEP * rate[f])
            return 0

        return body

    for step in range(STEPS):
        if step == 0:
            lax.fori_loop(2, blocks - 2, predict, 0)
            for copy in copies:
                copy.wait()
            for block in (0, 1, blocks - 2, blocks - 1):
                predict(block, 0)
        else:
            lax.fori_loop(0, blocks, predict, 0)
        if step < STEPS - 1:
            lax.fori_loop(0, blocks, correct(now, 0), 0)
        else:
            lax.fori_loop(1, blocks - 1, correct(fine, 16), 0)


def heun(state, size):
    fields, rows, width = state.shape
    vmem = pl.BlockSpec(memory_space=pltpu.VMEM)
    padded = pltpu.VMEM((fields, rows + 4 * HALO, width), jnp.float32)
    return pl.pallas_call(
        functools.partial(heun_kernel, size),
        out_shape=jax.ShapeDtypeStruct(state.shape, jnp.float32),
        in_specs=[vmem],
        out_specs=vmem,
        scratch_shapes=[padded, padded] + [pltpu.SemaphoreType.DMA((2,))] * 2,
        compiler_params=pltpu.CompilerParams(
            collective_id=0, has_side_effects=True, vmem_limit_bytes=8 << 20
        ),
        cost_estimate=pl.CostEstimate(
            flops=200 * rows * width, bytes_accessed=24 * rows * width, transcendentals=0
        ),
    )(state)


def apply_operator(s, a, b):
    (hr, hi), (ur, ui), (vr, vi) = s
    return (
        (a * ui + b * vi, -(a * ur + b * vr)),
        (a * hi + CORIOLIS * vr, CORIOLIS * vi - a * hr),
        (b * hi - CORIOLIS * ur, -(b * hr) - CORIOLIS * ui),
    )


def coarse_kernel(
    size, slices, fine, state, incoming, pairs, wide_h, wide_l, short_h, short_l,
    east, north, sine, versine, along_h, along_l, back_h, back_l, out,
    mine, theirs, gap, landed, acc, change, relayed, leaving, returned,
    ah, al, bh, bl, fetch, x_send, x_recv, y_send, y_recv, t_send, t_recv,
):
    fields, rows, nc = incoming.shape
    half = nc // 2
    count = half // size
    me, slot = lax.axis_index("space"), lax.axis_index("tm")
    peers = [lax.rem(me + d, size) for d in range(1, size)]
    origins = [lax.rem(me + size - d, size) for d in range(1, size)]
    following, previous = lax.rem(slot + 1, slices), lax.rem(slot + slices - 1, slices)

    fetches = [
        pltpu.make_async_copy(source, target, fetch.at[n])
        for n, (source, target) in enumerate(
            ((along_h, ah), (along_l, al), (back_h, bh), (back_l, bl))
        )
    ]
    for copy in fetches:
        copy.start()

    barrier = pltpu.get_barrier_semaphore()
    for peer in peers:
        pl.semaphore_signal(barrier, inc=1, device_id={"space": peer}, device_id_type=MESH)
    for other in (following, previous):
        pl.semaphore_signal(barrier, inc=1, device_id={"tm": other}, device_id_type=MESH)

    def to_space(source, target, send, recv, peer):
        return pltpu.make_async_remote_copy(
            src_ref=source, dst_ref=target, send_sem=send, recv_sem=recv,
            device_id={"space": peer}, device_id_type=MESH,
        )

    def to_next(source, target, n):
        return pltpu.make_async_remote_copy(
            src_ref=source, dst_ref=target, send_sem=t_send.at[n], recv_sem=t_recv.at[n],
            device_id={"tm": following}, device_id_type=MESH,
        )

    def spectra_of(stacked, high, low):
        up, down = split(stacked)
        return dot(high, up, (1, 1)) + (dot(high, down, (1, 1)) + dot(low, up, (1, 1)))

    def x_spectra(ref):
        parts = [split(ref[f]) for f in range(fields)]
        averaged = [dot(pairs[...], up) + dot(pairs[...], down) for up, down in parts]
        return spectra_of(jnp.concatenate(averaged, 0), wide_h[...], wide_l[...])

    def lay_out(value, put):
        for f in range(fields):
            both = value[:, f * rows : (f + 1) * rows]
            both = jnp.concatenate([both[:half], both[half:]], 1)
            for j in range(size):
                put(j, slice(f * count, (f + 1) * count), both[j * count : (j + 1) * count])

    def put_mine(j, at, value):
        mine[j, at] = value

    def put_gap(j, at, value):
        gap[j, at] = value

    lay_out(x_spectra(fine), put_mine)
    pl.semaphore_wait(barrier, len(peers) + 2)
    ahead = to_next(mine, theirs, 0)
    ahead.start()
    fresh = jnp.concatenate([incoming[f] for f in range(fields)], 0)
    fresh = spectra_of(fresh, short_h[...], short_l[...])
    drift = x_spectra(state) - jnp.where(slot == 0, fresh, 0.0)
    lay_out(-drift, put_gap)
    ahead.wait()
    for j in range(size):
        gap[j] = gap[j] + jnp.where(slot == 0, 0.0, theirs[j])

    copies = [
        to_space(gap.at[peer], landed.at[me], x_send.at[n], x_recv.at[n], peer)
        for n, peer in enumerate(peers)
    ]
    for copy in copies:
        copy.start()
    for copy in fetches:
        copy.wait()

    def y_spectra(block, at):
        up, down = split(block)
        return dot(up, ah[at]) + (dot(down, ah[at]) + dot(up, al[at]))

    acc[...] = y_spectra(gap[me], me)
    for copy, origin in zip(copies, origins):
        copy.wait_recv()
        acc[...] += y_spectra(landed[origin], origin)

    def propagate(more):
        for r in range(0, count, 8):
            at = slice(r, r + 8)
            state_of = []
            for f in range(fields):
                row = slice(f * count + r, f * count + r + 8)
                pair = [acc[row, :nc], acc[row, nc:]]
                if more is not None:
                    extra = (relayed[more, row, :nc], relayed[more, row, nc:])
                    pair = [p + jnp.where(slot == 0, 0.0, q) for p, q in zip(pair, extra)]
                state_of.append(pair)
            once = apply_operator(state_of, east[at], north[...])
            twice = apply_operator(once, east[at], north[...])
            for f in range(fields):
                row = slice(f * count + r, f * count + r + 8)
                for part, lanes in enumerate((slice(0, nc), slice(nc, 2 * nc))):
                    change[row, lanes] = (
                        state_of[f][part]
                        + sine[at] * once[f][part]
                        + versine[at] * twice[f][part]
                    )

    propagate(None)
    for n in range(slices - 1):
        ahead = to_next(change, relayed.at[n], 1 + n)
        ahead.start()
        ahead.wait()
        propagate(n)

    up, down = split(change[...])

    def y_fields(at):
        return dot(up, bh[at]) + (dot(down, bh[at]) + dot(up, bl[at]))

    home = []
    for n, peer in enumerate(peers):
        leaving[peer] = y_fields(peer)
        home.append(to_space(leaving.at[peer], returned.at[me], y_send.at[n], y_recv.at[n], peer))
        home[-1].start()
    out[me] = y_fields(me)
    for copy in copies:
        copy.wait_send()
    for copy, origin in zip(home, origins):
        copy.wait()
        out[origin] = returned[origin]


def shards(start_old, incoming):
    size, slices = lax.axis_size("space"), lax.axis_size("tm")
    state = start_old[0]
    width = state.shape[2]
    fields, rows, nc = incoming.shape
    half = nc // 2
    count = half // size
    forward, wide, along, back, inverse, wave, sine, versine = tables(nc, size)
    pairs = np.repeat(np.eye(rows, dtype=np.float32), RATIO, axis=1)

    fine = heun(state, size)

    first = lax.axis_index("space") * count
    cut = lambda a: lax.dynamic_slice_in_dim(jnp.asarray(a), first, count, 0)
    flat = lambda table: halves(table.reshape(nc, -1))
    back = back.reshape(2 * nc, size, 2 * rows).transpose(1, 0, 2)
    east = np.repeat(wave[:half, None], nc, axis=1)
    north = np.repeat(wave[None, :], 8, axis=0)
    operands = [fine, state, incoming, (0.5 * pairs).astype(jnp.bfloat16)]
    operands += [*flat(wide), *flat(forward), cut(east), north, cut(sine), cut(versine)]
    distant = [*halves(along.reshape(size, 2 * rows, 2 * nc)), *halves(back)]
    blocks = (size, fields * count, 2 * rows)
    whole = (fields * count, 2 * nc)
    shapes = [blocks] * 4 + [whole] * 2 + [(max(slices - 1, 1), *whole)] + [blocks] * 2
    vmem = pl.BlockSpec(memory_space=pltpu.VMEM)
    far = pl.BlockSpec(memory_space=pl.ANY)
    moved = pl.pallas_call(
        functools.partial(coarse_kernel, size, slices),
        out_shape=jax.ShapeDtypeStruct(blocks, jnp.float32),
        in_specs=[vmem] * len(operands) + [far] * len(distant),
        out_specs=vmem,
        scratch_shapes=[pltpu.VMEM(shape, jnp.float32) for shape in shapes]
        + [pltpu.VMEM(table.shape, jnp.bfloat16) for table in distant]
        + [pltpu.SemaphoreType.DMA((4,))]
        + [pltpu.SemaphoreType.DMA((size - 1,))] * 4
        + [pltpu.SemaphoreType.DMA((slices,))] * 2,
        compiler_params=pltpu.CompilerParams(
            collective_id=1, has_side_effects=True, vmem_limit_bytes=44 << 20
        ),
        cost_estimate=pl.CostEstimate(
            flops=40 * fields * count * nc * nc, bytes_accessed=32 * nc * nc, transcendentals=0
        ),
    )(*operands, *distant)

    moved = moved.reshape(size, fields, count, 2, rows).transpose(1, 4, 3, 0, 2)
    moved = moved.reshape(fields, rows, nc)
    matmul = functools.partial(
        jnp.einsum, precision=lax.Precision.HIGH, preferred_element_type=jnp.float32
    )
    moved = matmul("yY,fyk->fYk", pairs, moved)
    result = fine + matmul("fYk,kx->fYx", moved, inverse.reshape(nc, width))
    return result[None]


def solution(mesh):
    placed = (P(("group", "tm"), None, "space", None), P("group", "space", None))
    return jax.shard_map(
        shards,
        mesh=mesh,
        in_specs=placed,
        out_specs=P(("group", "tm"), None, "space", None),
        check_vma=False,
    )
```

```python
import functools
import math

import jax
import jax.numpy as jnp
import numpy as np
from jax import lax
from jax.experimental import pallas as pl
from jax.experimental.pallas import tpu as pltpu
from jax.sharding import PartitionSpec as P

RATIO = 2
STEPS = 2
TIME_STEP = 0.25
CORIOLIS = 0.5
HALO = 8
MESH = pl.DeviceIdType.MESH


def halves(table):
    high = table.astype(jnp.bfloat16)
    return high, (table - high.astype(np.float32)).astype(jnp.bfloat16)


def split(a):
    high = a.astype(jnp.bfloat16)
    return high, (a - high.astype(jnp.float32)).astype(jnp.bfloat16)


def dot(a, b, sides=(1, 0)):
    dims = (((sides[0],), (sides[1],)), ((), ()))
    return lax.dot_general(a, b, dims, preferred_element_type=jnp.float32)


def tables(nc, parts):
    half, rows = nc // 2, nc // parts
    x = np.arange(nc)
    angle = 2.0 * math.pi / nc * (np.outer(np.arange(half), x) % nc)
    real, imag = np.cos(angle), -np.sin(angle)
    imag[0] = (-1.0) ** x
    forward = np.stack([real, imag])
    wide = 0.5 * np.repeat(forward, RATIO, axis=2)

    angle = 2.0 * math.pi / nc * (np.outer(x, x) % nc)
    cos, sin = np.cos(angle), np.sin(angle)
    along = np.stack([np.stack([cos, -sin], 1), np.stack([sin, cos], 1)])
    back = np.stack([np.stack([cos, sin], 1), np.stack([-sin, cos], 1)])
    along = along.reshape(2, parts, rows, 2 * nc).transpose(1, 0, 2, 3).reshape(2 * nc, 2 * nc)
    back = back.reshape(2 * nc, 2, parts, rows).transpose(0, 2, 1, 3).reshape(2 * nc, 2 * nc)

    scale = np.full((1, half, 1), 2.0 / (nc * nc))
    scale[:, 0] = 1.0 / (nc * nc)
    inverse = np.repeat(forward * scale, RATIO, axis=2)

    index = np.where(x < half, x, x - nc)
    index = np.where(x == half, 0, index)
    wave = index * (2.0 * math.pi / (nc * RATIO))
    omega = np.sqrt(CORIOLIS**2 + wave[:half, None] ** 2 + wave[None, :] ** 2)
    duration = STEPS * TIME_STEP
    sine = np.sin(omega * duration) / omega
    versine = (1.0 - np.cos(omega * duration)) / omega**2
    single = lambda a: np.asarray(a, np.float32)
    return [single(a) for a in (forward, wide, along, back, inverse, wave, sine, versine)]


def tendency(window):
    width = window[0].shape[-1]
    mid = [a[8:16] for a in window]
    south = [a[7:15] for a in window]
    north = [a[9:17] for a in window]
    west = [pltpu.roll(a, 1, 1) for a in mid]
    east = [pltpu.roll(a, width - 1, 1) for a in mid]
    _, u, v = mid
    flux = (1.0 + east[0]) * east[1] - (1.0 + west[0]) * west[1]
    flux = flux + ((1.0 + north[0]) * north[2] - (1.0 + south[0]) * south[2])
    half_u, half_v = 0.5 * u, 0.5 * v
    rate_u = CORIOLIS * v - (
        half_u * (east[1] - west[1]) + half_v * (north[1] - south[1]) + 0.5 * (east[0] - west[0])
    )
    rate_v = -(CORIOLIS * u) - (
        half_u * (east[2] - west[2]) + half_v * (north[2] - south[2]) + 0.5 * (north[0] - south[0])
    )
    return mid, (-0.5 * flux, rate_u, rate_v)


def rows_at(row):
    return row if isinstance(row, int) else pl.multiple_of(row, 8)


def heun(state, fine, now, first, exchange_rims):
    rows = state.shape[1]
    blocks = (rows + 2 * HALO) // 8
    pad = jnp.zeros((HALO, state.shape[2]), jnp.float32)
    for f in range(3):
        now[f, 16 : 16 + rows] = state[f]
        for ref in (now, first):
            ref[f, 0:8] = pad
            ref[f, 24 + rows : 32 + rows] = pad

    def window(ref, block):
        at = rows_at(block * 8)
        return [ref[f, pl.ds(at, 24)] for f in range(3)]

    def predict(block, _):
        mid, rate = tendency(window(now, block))
        at = rows_at(block * 8 + 8)
        for f in range(3):
            first[f, pl.ds(at, 8)] = mid[f] + TIME_STEP * rate[f]
        return 0

    def correct(out, shift):
        def body(block, _):
            mid, rate = tendency(window(first, block))
            at = rows_at(block * 8 + 8)
            to = rows_at(block * 8 + 8 - shift)
            for f in range(3):
                out[f, pl.ds(to, 8)] = 0.5 * (now[f, pl.ds(at, 8)] + mid[f] + TIME_STEP * rate[f])
            return 0

        return body

    for step in range(STEPS):
        if step == 0:
            lax.fori_loop(2, blocks - 2, predict, 0)
            exchange_rims()
            for block in (0, 1, blocks - 2, blocks - 1):
                predict(block, 0)
        else:
            lax.fori_loop(0, blocks, predict, 0)
        if step < STEPS - 1:
            lax.fori_loop(0, blocks, correct(now, 0), 0)
        else:
            lax.fori_loop(1, blocks - 1, correct(fine, 16), 0)


def apply_operator(s, a, b):
    (hr, hi), (ur, ui), (vr, vi) = s
    return (
        (a * ui + b * vi, -(a * ur + b * vr)),
        (a * hi + CORIOLIS * vr, CORIOLIS * vi - a * hr),
        (b * hi - CORIOLIS * ur, -(b * hr) - CORIOLIS * ui),
    )


def kernel(
    size, slices, state, incoming, pairs, north,
    wide_h_far, wide_l_far, short_h_far, short_l_far, along_h, along_l, back_h, back_l,
    east_far, sine_far, versine_far, fine, out,
    now, first, mine, theirs, gap, landed, acc, change, relayed, leaving, returned,
    east, sine, versine, wide_h, wide_l, short_h, short_l, ah, al, bh, bl,
    fetch, x_send, x_recv, y_send, y_recv, t_send, t_recv, rim_send, rim_recv,
):
    fields, rows, nc = incoming.shape
    half = nc // 2
    count = half // size
    me, slot = lax.axis_index("space"), lax.axis_index("tm")
    peers = [lax.rem(me + d, size) for d in range(1, size)]
    origins = [lax.rem(me + size - d, size) for d in range(1, size)]
    following, previous = lax.rem(slot + 1, slices), lax.rem(slot + slices - 1, slices)

    share = pl.ds(pl.multiple_of(me * count, count), count)
    fetches = [
        pltpu.make_async_copy(source, target, fetch.at[n])
        for n, (source, target) in enumerate(
            (
                (wide_h_far, wide_h),
                (wide_l_far, wide_l),
                (short_h_far, short_h),
                (short_l_far, short_l),
                (along_h, ah),
                (along_l, al),
                (east_far.at[share], east),
                (sine_far.at[share], sine),
                (versine_far.at[share], versine),
                (back_h, bh),
                (back_l, bl),
            )
        )
    ]
    for copy in fetches:
        copy.start()

    barrier = pltpu.get_barrier_semaphore()
    for peer in peers:
        pl.semaphore_signal(barrier, inc=1, device_id={"space": peer}, device_id_type=MESH)
    for other in (following, previous):
        pl.semaphore_signal(barrier, inc=1, device_id={"tm": other}, device_id_type=MESH)

    def to_space(source, target, send, recv, peer):
        return pltpu.make_async_remote_copy(
            src_ref=source, dst_ref=target, send_sem=send, recv_sem=recv,
            device_id={"space": peer}, device_id_type=MESH,
        )

    def to_next(source, target, n):
        return pltpu.make_async_remote_copy(
            src_ref=source, dst_ref=target, send_sem=t_send.at[n], recv_sem=t_recv.at[n],
            device_id={"tm": following}, device_id_type=MESH,
        )

    def spectra_of(stacked, high, low):
        up, down = split(stacked)
        return dot(high, up, (1, 1)) + (dot(high, down, (1, 1)) + dot(low, up, (1, 1)))

    def x_spectra(ref):
        parts = [split(ref[f]) for f in range(fields)]
        averaged = [dot(pairs[...], up) + dot(pairs[...], down) for up, down in parts]
        return spectra_of(jnp.concatenate(averaged, 0), wide_h[...], wide_l[...])

    def lay_out(value, put):
        for f in range(fields):
            both = value[:, f * rows : (f + 1) * rows]
            both = jnp.concatenate([both[:half], both[half:]], 1)
            for j in range(size):
                put(j, slice(f * count, (f + 1) * count), both[j * count : (j + 1) * count])

    def put_mine(j, at, value):
        mine[j, at] = value

    def put_gap(j, at, value):
        gap[j, at] = value

    copies = [
        to_space(gap.at[peer], landed.at[me], x_send.at[n], x_recv.at[n], peer)
        for n, peer in enumerate(peers)
    ]
    wide_rows = state.shape[1]
    rims = [
        to_space(
            state.at[:, pl.ds(source, HALO)], now.at[:, pl.ds(target, HALO)],
            rim_send.at[n], rim_recv.at[n], peer,
        )
        for n, (source, target, peer) in enumerate(
            ((wide_rows - HALO, 8, peers[0]), (0, 16 + wide_rows, peers[-1]))
        )
    ]

    def exchange_rims():
        pl.semaphore_wait(barrier, len(peers) + 2)
        for copy in rims:
            copy.start()
        for copy in fetches[:4]:
            copy.wait()
        fresh = jnp.concatenate([incoming[f] for f in range(fields)], 0)
        fresh = spectra_of(fresh, short_h[...], short_l[...])
        drift = x_spectra(state) - jnp.where(slot == 0, fresh, 0.0)
        lay_out(-drift, put_gap)
        for copy in rims:
            copy.wait()

        @pl.when(slot == 0)
        def _():
            for copy in copies:
                copy.start()

    heun(state, fine, now, first, exchange_rims)
    lay_out(x_spectra(fine), put_mine)
    ahead = to_next(mine, theirs, 0)

    @pl.when(slot < slices - 1)
    def _():
        ahead.start()

    for copy in fetches[4:]:
        copy.wait()

    @pl.when(slot > 0)
    def _():
        ahead.wait_recv()
        for j in range(size):
            gap[j] = gap[j] + theirs[j]
        for copy in copies:
            copy.start()

    def y_spectra(block, at):
        up, down = split(block)
        return dot(up, ah[at]) + (dot(down, ah[at]) + dot(up, al[at]))

    acc[...] = y_spectra(gap[me], me)
    for copy, origin in zip(copies, origins):
        copy.wait_recv()
        acc[...] += y_spectra(landed[origin], origin)

    relay = to_next(change, relayed, 1)

    @pl.when(slot > 0)
    def _():
        relay.wait_recv()
        acc[...] += relayed[...]

    for r in range(0, count, 8):
        at = slice(r, r + 8)
        places = [slice(f * count + r, f * count + r + 8) for f in range(fields)]
        spectra = [(acc[row, :nc], acc[row, nc:]) for row in places]
        once = apply_operator(spectra, east[at], north[...])
        twice = apply_operator(once, east[at], north[...])
        for f, row in enumerate(places):
            for part, lanes in enumerate((slice(0, nc), slice(nc, 2 * nc))):
                change[row, lanes] = (
                    spectra[f][part] + sine[at] * once[f][part] + versine[at] * twice[f][part]
                )

    @pl.when(slot < slices - 1)
    def _():
        relay.start()

    up, down = split(change[...])

    def y_fields(at):
        return dot(up, bh[at]) + (dot(down, bh[at]) + dot(up, bl[at]))

    home = []
    for n, peer in enumerate(peers):
        leaving[peer] = y_fields(peer)
        home.append(to_space(leaving.at[peer], returned.at[me], y_send.at[n], y_recv.at[n], peer))
        home[-1].start()
    out[me] = y_fields(me)
    for copy in copies:
        copy.wait_send()

    @pl.when(slot < slices - 1)
    def _():
        ahead.wait_send()
        relay.wait_send()

    for copy, origin in zip(home, origins):
        copy.wait()
        out[origin] = returned[origin]


def shards(start_old, incoming):
    size, slices = lax.axis_size("space"), lax.axis_size("tm")
    state = start_old[0]
    width = state.shape[2]
    fields, rows, nc = incoming.shape
    half = nc // 2
    count = half // size
    forward, wide, along, back, inverse, wave, sine, versine = tables(nc, size)
    pairs = np.repeat(np.eye(rows, dtype=np.float32), RATIO, axis=1)

    flat = lambda table: halves(table.reshape(nc, -1))
    back = back.reshape(2 * nc, size, 2 * rows).transpose(1, 0, 2)
    east = np.repeat(wave[:half, None], nc, axis=1)
    north = np.repeat(wave[None, :], 8, axis=0)
    operands = [state, incoming, (0.5 * pairs).astype(jnp.bfloat16), north]
    distant = [*flat(wide), *flat(forward)]
    distant += [*halves(along.reshape(size, 2 * rows, 2 * nc)), *halves(back)]
    blocks = (size, fields * count, 2 * rows)
    whole = (fields * count, 2 * nc)
    padded = (fields, state.shape[1] + 4 * HALO, width)
    shapes = [padded] * 2 + [blocks] * 4 + [whole] * 3 + [blocks] * 2 + [(count, nc)] * 3
    vmem = pl.BlockSpec(memory_space=pltpu.VMEM)
    far = pl.BlockSpec(memory_space=pl.ANY)
    fine, moved = pl.pallas_call(
        functools.partial(kernel, size, slices),
        out_shape=[jax.ShapeDtypeStruct(shape, jnp.float32) for shape in (state.shape, blocks)],
        in_specs=[vmem] * len(operands) + [far] * (len(distant) + 3),
        out_specs=[vmem] * 2,
        scratch_shapes=[pltpu.VMEM(shape, jnp.float32) for shape in shapes]
        + [pltpu.VMEM(table.shape, jnp.bfloat16) for table in distant]
        + [pltpu.SemaphoreType.DMA((len(distant) + 3,))]
        + [pltpu.SemaphoreType.DMA((size - 1,))] * 4
        + [pltpu.SemaphoreType.DMA((2,))] * 4,
        compiler_params=pltpu.CompilerParams(
            collective_id=0, has_side_effects=True, vmem_limit_bytes=48 << 20
        ),
        cost_estimate=pl.CostEstimate(
            flops=40 * fields * count * nc * nc, bytes_accessed=32 * nc * nc, transcendentals=0
        ),
    )(*operands, *distant, east, sine, versine)

    moved = moved.reshape(size, fields, count, 2, rows).transpose(1, 4, 3, 0, 2)
    moved = moved.reshape(fields, rows, nc)
    matmul = functools.partial(
        jnp.einsum, precision=lax.Precision.HIGH, preferred_element_type=jnp.float32
    )
    moved = matmul("yY,fyk->fYk", pairs, moved)
    result = fine + matmul("fYk,kx->fYx", moved, inverse.reshape(nc, width))
    return result[None]


def solution(mesh):
    placed = (P(("group", "tm"), None, "space", None), P("group", "space", None))
    return jax.shard_map(
        shards,
        mesh=mesh,
        in_specs=placed,
        out_specs=P(("group", "tm"), None, "space", None),
        check_vma=False,
    )
```

```python
import functools
import math

import jax
import jax.numpy as jnp
import numpy as np
from jax import lax
from jax.experimental import pallas as pl
from jax.experimental.pallas import tpu as pltpu
from jax.sharding import PartitionSpec as P

RATIO = 2
STEPS = 2
TIME_STEP = 0.25
CORIOLIS = 0.5
HALO = 8
MESH = pl.DeviceIdType.MESH


def halves(table):
    high = table.astype(jnp.bfloat16)
    return high, (table - high.astype(np.float32)).astype(jnp.bfloat16)


def split(a):
    high = a.astype(jnp.bfloat16)
    return high, (a - high.astype(jnp.float32)).astype(jnp.bfloat16)


def dot(a, b, sides=(1, 0)):
    dims = (((sides[0],), (sides[1],)), ((), ()))
    return lax.dot_general(a, b, dims, preferred_element_type=jnp.float32)


def tables(nc, parts):
    half, rows = nc // 2, nc // parts
    x = np.arange(nc)
    angle = 2.0 * math.pi / nc * (np.outer(np.arange(half), x) % nc)
    real, imag = np.cos(angle), -np.sin(angle)
    imag[0] = (-1.0) ** x
    forward = np.stack([real, imag])
    wide = 0.5 * np.repeat(forward, RATIO, axis=2)

    angle = 2.0 * math.pi / nc * (np.outer(x, x) % nc)
    cos, sin = np.cos(angle), np.sin(angle)
    along = np.stack([np.stack([cos, -sin], 1), np.stack([sin, cos], 1)])
    back = np.stack([np.stack([cos, sin], 1), np.stack([-sin, cos], 1)])
    along = along.reshape(2, parts, rows, 2 * nc).transpose(1, 0, 2, 3).reshape(2 * nc, 2 * nc)
    back = back.reshape(2 * nc, 2, parts, rows).transpose(0, 2, 1, 3).reshape(2 * nc, 2 * nc)

    scale = np.full((1, half, 1), 2.0 / (nc * nc))
    scale[:, 0] = 1.0 / (nc * nc)
    inverse = np.repeat(forward * scale, RATIO, axis=2)

    index = np.where(x < half, x, x - nc)
    index = np.where(x == half, 0, index)
    wave = index * (2.0 * math.pi / (nc * RATIO))
    omega = np.sqrt(CORIOLIS**2 + wave[:half, None] ** 2 + wave[None, :] ** 2)
    duration = STEPS * TIME_STEP
    sine = np.sin(omega * duration) / omega
    versine = (1.0 - np.cos(omega * duration)) / omega**2
    single = lambda a: np.asarray(a, np.float32)
    return [single(a) for a in (forward, wide, along, back, inverse, wave, sine, versine)]


def tendency(window):
    width = window[0].shape[-1]
    mid = [a[8:16] for a in window]
    south = [a[7:15] for a in window]
    north = [a[9:17] for a in window]
    west = [pltpu.roll(a, 1, 1) for a in mid]
    east = [pltpu.roll(a, width - 1, 1) for a in mid]
    _, u, v = mid
    flux = (1.0 + east[0]) * east[1] - (1.0 + west[0]) * west[1]
    flux = flux + ((1.0 + north[0]) * north[2] - (1.0 + south[0]) * south[2])
    half_u, half_v = 0.5 * u, 0.5 * v
    rate_u = CORIOLIS * v - (
        half_u * (east[1] - west[1]) + half_v * (north[1] - south[1]) + 0.5 * (east[0] - west[0])
    )
    rate_v = -(CORIOLIS * u) - (
        half_u * (east[2] - west[2]) + half_v * (north[2] - south[2]) + 0.5 * (north[0] - south[0])
    )
    return mid, (-0.5 * flux, rate_u, rate_v)


def rows_at(row):
    return row if isinstance(row, int) else pl.multiple_of(row, 8)


def heun(fine, now, first, exchange_rims):
    rows, width = fine.shape[1:]
    blocks = (rows + 2 * HALO) // 8
    pad = jnp.zeros((HALO, width), jnp.float32)
    for f in range(3):
        for ref in (now, first):
            ref[f, 0:8] = pad
            ref[f, 24 + rows : 32 + rows] = pad

    def window(ref, block):
        at = rows_at(block * 8)
        return [ref[f, pl.ds(at, 24)] for f in range(3)]

    def predict(block, _):
        mid, rate = tendency(window(now, block))
        at = rows_at(block * 8 + 8)
        for f in range(3):
            first[f, pl.ds(at, 8)] = mid[f] + TIME_STEP * rate[f]
        return 0

    def correct(out, shift):
        def body(block, _):
            mid, rate = tendency(window(first, block))
            at = rows_at(block * 8 + 8)
            to = rows_at(block * 8 + 8 - shift)
            for f in range(3):
                out[f, pl.ds(to, 8)] = 0.5 * (now[f, pl.ds(at, 8)] + mid[f] + TIME_STEP * rate[f])
            return 0

        return body

    for step in range(STEPS):
        if step == 0:
            lax.fori_loop(2, blocks - 2, predict, 0)
            exchange_rims()
            for block in (0, 1, blocks - 2, blocks - 1):
                predict(block, 0)
        else:
            lax.fori_loop(0, blocks, predict, 0)
        if step < STEPS - 1:
            lax.fori_loop(0, blocks, correct(now, 0), 0)
        else:
            lax.fori_loop(1, blocks - 1, correct(fine, 16), 0)


def apply_operator(s, a, b):
    (hr, hi), (ur, ui), (vr, vi) = s
    return (
        (a * ui + b * vi, -(a * ur + b * vr)),
        (a * hi + CORIOLIS * vr, CORIOLIS * vi - a * hr),
        (b * hi - CORIOLIS * ur, -(b * hr) - CORIOLIS * ui),
    )


def kernel(
    size, slices, state, incoming_far, pairs_far, north_far,
    wide_h_far, wide_l_far, short_h_far, short_l_far, along_h, along_l, back_h, back_l,
    east_far, sine_far, versine_far, fine, out,
    incoming, north, pairs, now, first, mine, theirs, gap, landed, acc, change, relayed, leaving, returned,
    east, sine, versine, wide_h, wide_l, short_h, short_l, ah, al, bh, bl,
    fetch, x_send, x_recv, y_send, y_recv, t_send, t_recv, rim_send, rim_recv,
):
    fields, rows, nc = incoming_far.shape
    half = nc // 2
    count = half // size
    me, slot = lax.axis_index("space"), lax.axis_index("tm")
    peers = [lax.rem(me + d, size) for d in range(1, size)]
    origins = [lax.rem(me + size - d, size) for d in range(1, size)]
    following, previous = lax.rem(slot + 1, slices), lax.rem(slot + slices - 1, slices)

    share = pl.ds(pl.multiple_of(me * count, count), count)
    fetches = [
        pltpu.make_async_copy(source, target, fetch.at[n])
        for n, (source, target) in enumerate(
            (
                (state, now.at[:, pl.ds(16, state.shape[1])]),
                (incoming_far, incoming),
                (pairs_far, pairs),
                (wide_h_far, wide_h),
                (wide_l_far, wide_l),
                (short_h_far, short_h),
                (short_l_far, short_l),
                (along_h, ah),
                (along_l, al),
                (east_far.at[share], east),
                (sine_far.at[share], sine),
                (versine_far.at[share], versine),
                (north_far, north),
                (back_h, bh),
                (back_l, bl),
            )
        )
    ]
    for copy in fetches:
        copy.start()

    barrier = pltpu.get_barrier_semaphore()
    for peer in peers:
        pl.semaphore_signal(barrier, inc=1, device_id={"space": peer}, device_id_type=MESH)
    for other in (following, previous):
        pl.semaphore_signal(barrier, inc=1, device_id={"tm": other}, device_id_type=MESH)

    def to_space(source, target, send, recv, peer):
        return pltpu.make_async_remote_copy(
            src_ref=source, dst_ref=target, send_sem=send, recv_sem=recv,
            device_id={"space": peer}, device_id_type=MESH,
        )

    def to_next(source, target, n):
        return pltpu.make_async_remote_copy(
            src_ref=source, dst_ref=target, send_sem=t_send.at[n], recv_sem=t_recv.at[n],
            device_id={"tm": following}, device_id_type=MESH,
        )

    def spectra_of(stacked, high, low):
        up, down = split(stacked)
        return dot(high, up, (1, 1)) + (dot(high, down, (1, 1)) + dot(low, up, (1, 1)))

    def x_spectra(ref):
        parts = [split(ref[f]) for f in range(fields)]
        averaged = [dot(pairs[...], up) + dot(pairs[...], down) for up, down in parts]
        return spectra_of(jnp.concatenate(averaged, 0), wide_h[...], wide_l[...])

    def lay_out(value, put):
        for f in range(fields):
            both = value[:, f * rows : (f + 1) * rows]
            both = jnp.concatenate([both[:half], both[half:]], 1)
            for j in range(size):
                put(j, slice(f * count, (f + 1) * count), both[j * count : (j + 1) * count])

    def put_mine(j, at, value):
        mine[j, at] = value

    def put_gap(j, at, value):
        gap[j, at] = value

    copies = [
        to_space(gap.at[peer], landed.at[me], x_send.at[n], x_recv.at[n], peer)
        for n, peer in enumerate(peers)
    ]
    wide_rows = state.shape[1]
    rims = [
        to_space(
            state.at[:, pl.ds(source, HALO)], now.at[:, pl.ds(target, HALO)],
            rim_send.at[n], rim_recv.at[n], peer,
        )
        for n, (source, target, peer) in enumerate(
            ((wide_rows - HALO, 8, peers[0]), (0, 16 + wide_rows, peers[-1]))
        )
    ]

    def exchange_rims():
        pl.semaphore_wait(barrier, len(peers) + 2)
        for copy in rims:
            copy.start()
        for copy in fetches[1:7]:
            copy.wait()
        fresh = jnp.concatenate([incoming[f] for f in range(fields)], 0)
        fresh = spectra_of(fresh, short_h[...], short_l[...])
        drift = x_spectra(now.at[:, pl.ds(16, wide_rows)]) - jnp.where(slot == 0, fresh, 0.0)
        lay_out(-drift, put_gap)
        for copy in rims:
            copy.wait()

        @pl.when(slot == 0)
        def _():
            for copy in copies:
                copy.start()

    fetches[0].wait()
    heun(fine, now, first, exchange_rims)
    lay_out(x_spectra(fine), put_mine)
    ahead = to_next(mine, theirs, 0)

    @pl.when(slot < slices - 1)
    def _():
        ahead.start()

    for copy in fetches[7:]:
        copy.wait()

    @pl.when(slot > 0)
    def _():
        ahead.wait_recv()
        for j in range(size):
            gap[j] = gap[j] + theirs[j]
        for copy in copies:
            copy.start()

    def y_spectra(block, at):
        up, down = split(block)
        return dot(up, ah[at]) + (dot(down, ah[at]) + dot(up, al[at]))

    acc[...] = y_spectra(gap[me], me)
    for copy, origin in zip(copies, origins):
        copy.wait_recv()
        acc[...] += y_spectra(landed[origin], origin)

    relay = to_next(change, relayed, 1)

    @pl.when(slot > 0)
    def _():
        relay.wait_recv()
        acc[...] += relayed[...]

    for r in range(0, count, 8):
        at = slice(r, r + 8)
        places = [slice(f * count + r, f * count + r + 8) for f in range(fields)]
        spectra = [(acc[row, :nc], acc[row, nc:]) for row in places]
        once = apply_operator(spectra, east[at], north[...])
        twice = apply_operator(once, east[at], north[...])
        for f, row in enumerate(places):
            for part, lanes in enumerate((slice(0, nc), slice(nc, 2 * nc))):
                change[row, lanes] = (
                    spectra[f][part] + sine[at] * once[f][part] + versine[at] * twice[f][part]
                )

    @pl.when(slot < slices - 1)
    def _():
        relay.start()

    up, down = split(change[...])

    def y_fields(at):
        return dot(up, bh[at]) + (dot(down, bh[at]) + dot(up, bl[at]))

    home = []
    for n, peer in enumerate(peers):
        leaving[peer] = y_fields(peer)
        home.append(to_space(leaving.at[peer], returned.at[me], y_send.at[n], y_recv.at[n], peer))
        home[-1].start()
    out[me] = y_fields(me)
    for copy in copies:
        copy.wait_send()

    @pl.when(slot < slices - 1)
    def _():
        ahead.wait_send()
        relay.wait_send()

    for copy, origin in zip(home, origins):
        copy.wait()
        out[origin] = returned[origin]


def shards(start_old, incoming):
    size, slices = lax.axis_size("space"), lax.axis_size("tm")
    state = start_old[0]
    width = state.shape[2]
    fields, rows, nc = incoming.shape
    half = nc // 2
    count = half // size
    forward, wide, along, back, inverse, wave, sine, versine = tables(nc, size)
    pairs = np.repeat(np.eye(rows, dtype=np.float32), RATIO, axis=1)

    flat = lambda table: halves(table.reshape(nc, -1))
    back = back.reshape(2 * nc, size, 2 * rows).transpose(1, 0, 2)
    east = np.repeat(wave[:half, None], nc, axis=1)
    north = np.repeat(wave[None, :], 8, axis=0)
    operands = [state, incoming, (0.5 * pairs).astype(jnp.bfloat16), north]
    distant = [*flat(wide), *flat(forward)]
    distant += [*halves(along.reshape(size, 2 * rows, 2 * nc)), *halves(back)]
    blocks = (size, fields * count, 2 * rows)
    whole = (fields * count, 2 * nc)
    padded = (fields, state.shape[1] + 4 * HALO, width)
    shapes = [incoming.shape, north.shape] + [padded] * 2 + [blocks] * 4 + [whole] * 3 + [blocks] * 2 + [(count, nc)] * 3
    buffers = [pltpu.VMEM(shape, jnp.float32) for shape in shapes]
    buffers[2:2] = [pltpu.VMEM(operands[2].shape, jnp.bfloat16)]
    vmem = pl.BlockSpec(memory_space=pltpu.VMEM)
    far = pl.BlockSpec(memory_space=pltpu.HBM)
    fine, moved = pl.pallas_call(
        functools.partial(kernel, size, slices),
        out_shape=[jax.ShapeDtypeStruct(shape, jnp.float32) for shape in (state.shape, blocks)],
        in_specs=[far] * (len(operands) + len(distant) + 3),
        out_specs=[vmem] * 2,
        scratch_shapes=buffers
        + [pltpu.VMEM(table.shape, jnp.bfloat16) for table in distant]
        + [pltpu.SemaphoreType.DMA((len(operands) + len(distant) + 3,))]
        + [pltpu.SemaphoreType.DMA((size - 1,))] * 4
        + [pltpu.SemaphoreType.DMA((2,))] * 4,
        compiler_params=pltpu.CompilerParams(
            collective_id=0, has_side_effects=True, vmem_limit_bytes=(64 << 20) - (128 << 10)
        ),
        cost_estimate=pl.CostEstimate(
            flops=40 * fields * count * nc * nc, bytes_accessed=32 * nc * nc, transcendentals=0
        ),
    )(*operands, *distant, east, sine, versine)

    moved = moved.reshape(size, fields, count, 2, rows).transpose(1, 4, 3, 0, 2)
    moved = moved.reshape(fields, rows, nc)
    matmul = functools.partial(
        jnp.einsum, precision=lax.Precision.HIGH, preferred_element_type=jnp.float32
    )
    moved = matmul("yY,fyk->fYk", pairs, moved)
    result = fine + matmul("fYk,kx->fYx", moved, inverse.reshape(nc, width))
    return result[None]


def solution(mesh):
    placed = (P(("group", "tm"), None, "space", None), P("group", "space", None))
    return jax.shard_map(
        shards,
        mesh=mesh,
        in_specs=placed,
        out_specs=P(("group", "tm"), None, "space", None),
        check_vma=False,
    )
```
